32 devices in a mesh: groups: 2 (over y), tok: 4 (over z), col: 2 (over x), head: 2 (over core).
Axes of the slice: x: 2, y: 2, z: 4, core: 2. Of those that a mesh axis runs over, the one named last changes fastest.
Arguments:
- latents: bfloat16 [4, 8192, 512], P(('groups', 'col'), ('tok', 'head')), parts along dimension 0, may hold values from -110 to 110
- weights: bfloat16 [2, 512, 32768], P(None, None, ('tok', 'head')), may hold values from -0.25 to 0.25
- start_basis: bfloat16 [32768, 256], P(('tok', 'head')), may hold values from -6 to 6
- layer_pick: int32 [4, 128], P('groups'), parts along dimension 0, may hold values from 0 to 1
Outputs:
- basis: float32 [4, 32768, 256], P(('groups', 'col'), ('tok', 'head')), parts along dimension 0
- core: float32 [4, 512, 256], P(('groups', 'col')), parts along dimension 0
The draws below stay inside these ranges and needn't reach their ends.
There are 2 independent parts, one for each index of `groups`. The reference program is written for one: setup_inputs(seed, part) draws one part's arguments, and reference() takes and returns one part's arrays. A program takes and returns all parts, laid end to end along the dimension named above; an argument that names none is the same for every part. Nothing has to cross between parts.
Inputs may be any that keep to these rules, and one draw needn't show every extreme that they name: `layer_pick`: a layer of the stack for each head of each layer slot.
All inputs are finite; a program needn't handle non-finite values.
Results may differ from the reference program's by a relative error of at most 0.0003.
Values sent between devices are 32-bit elements; how exact they have to be, the bound alone decides.
A program may use at most 128 MiB of HBM per device.

```python
import math
import jax
import jax.numpy as jnp
from jax import lax

D = 512
OUT = 32768
HEADS = 128
RANK = 256
STEPS = 2
TOK_DEV = 1024
LAYERS = 2
HEAD_OUT = 256
TOKENS = 8192


def draw_latents(key, part):
    key = jax.random.fold_in(key, 11)
    key_base, key_col, key_row = jax.random.split(key, 3)
    col_scale = jnp.exp(jax.random.uniform(key_col, (1, 1, D), jnp.float32, 0.0, 2.3026))
    row_scale = jnp.exp(jax.random.uniform(key_row, (LAYERS, TOKENS, 1), jnp.float32, 0.0, 2.3026))
    blocks = TOKENS // TOK_DEV
    position = (jnp.arange(TOKENS) // TOK_DEV).astype(jnp.float32) / max(blocks - 1, 1)
    rising = jnp.sqrt(3.0 ** position).reshape(1, TOKENS, 1)
    base = jnp.clip(jax.random.normal(key_base, (LAYERS, TOKENS, D), jnp.float32), -6.0, 6.0)
    return (0.1 * base * row_scale * col_scale * rising).astype(jnp.bfloat16)


def with_ends(values, key, smallest, top_value):
    index_at = [jax.random.randint(jax.random.fold_in(key, axis), (), 0, length) for axis, length in enumerate(values.shape)]
    longest = values.shape.index(max(values.shape))
    next_to = index_at[:longest] + [(index_at[longest] + 1) % values.shape[longest]] + index_at[longest + 1:]
    return values.at[tuple(index_at)].set(smallest).at[tuple(next_to)].set(top_value)


def steps_of(own_key, shape, cuts, smallest, largest):
    def one(axis_at, blocks):
        draws = jax.random.uniform(jax.random.fold_in(jax.random.fold_in(own_key, 6), axis_at), (blocks,), jnp.float32, smallest / len(cuts), largest / len(cuts))
        return jnp.repeat(jnp.exp(draws), shape[axis_at] // blocks).reshape((-1,) + (1,) * (len(shape) - axis_at - 1))

    gain = one(*cuts[0])
    for cut in cuts[1:]:
        gain = gain * one(*cut)
    return gain


def noise(own_key, shape, deviation, most, shards=(), held_as=jnp.bfloat16):
    loudness = steps_of(own_key, shape, shards, -0.22, 0.18) if shards else 1.0
    drawn = jax.random.normal(own_key, shape, jnp.float32) * deviation * loudness
    return jnp.minimum(jnp.maximum(drawn, -most), most).astype(held_as)


def setup_inputs(seed: int = 0, part: int = 0) -> dict:
    keys = jax.random.split(jax.random.key(seed), 5)
    part_splits = jax.random.split(jax.random.fold_in(keys[4], part), 5)
    latents = draw_latents(jax.random.fold_in(jax.random.fold_in(keys[4], part), 71), part)
    weights = noise(keys[1], (LAYERS, D, OUT), D ** -0.5, 0.25, ((2, 8),))
    start_basis = noise(keys[2], (OUT, RANK), 1.0, 6.0, ((0, 8),))
    layer_pick = with_ends(jax.random.randint(part_splits[3], (LAYERS, HEADS), 0, LAYERS), jax.random.fold_in(part_splits[3], 1), 0, LAYERS - 1).astype(jnp.int32)
    return dict(latents=latents, weights=weights, start_basis=start_basis, layer_pick=layer_pick)


def product(left, right):
    return jnp.dot(left, right, precision=lax.Precision.HIGHEST)

def orthonormal(block):
    lower = jnp.linalg.cholesky(product(block.T, block))
    return lax.linalg.triangular_solve(lower, block, left_side=False, lower=True, transpose_a=True)

def reference(latents, weights, start_basis, layer_pick):
    bases = []
    cores = []
    stacked = weights.reshape(LAYERS, D, HEADS, HEAD_OUT)
    head_index = jnp.arange(HEADS, dtype=jnp.int32)
    for layer in range(LAYERS):
        act = latents[layer]
        gram = jnp.dot(act.T.astype(jnp.float32), act.astype(jnp.float32), preferred_element_type=jnp.float32)
        upper = jnp.linalg.cholesky(gram).T
        chosen = stacked[layer_pick[layer].astype(jnp.int32), :, head_index, :]
        weight = jnp.transpose(chosen, (1, 0, 2)).reshape(D, OUT).astype(jnp.float32)
        current = start_basis.astype(jnp.float32)
        for step in range(STEPS):
            image = product(upper, product(weight, current))
            left = orthonormal(image)
            back = product(weight.T, product(upper.T, left))
            current = orthonormal(back)
        cores.append(product(weight, current))
        bases.append(current * math.sqrt(OUT))
    return (jnp.stack(bases), jnp.stack(cores))
```

```python
import math

import jax
import jax.numpy as jnp
from jax import lax
from jax.sharding import PartitionSpec as P

OUT = 32768
STEPS = 2
HEAD_OUT = 256


def product(left, right):
    return jnp.dot(left, right, precision=lax.Precision.HIGHEST)


def chosen_weight(weights, layer_pick):
    stack_count, _, col_count = weights.shape
    heads_here = col_count // HEAD_OUT
    slot = lax.axis_index("col")
    first_head = lax.axis_index(("tok", "head")) * heads_here
    picks = lax.dynamic_slice_in_dim(layer_pick[slot], first_head, heads_here, 0)
    pick_of_col = jnp.repeat(picks, HEAD_OUT)[None]
    weight = weights[0]
    for layer in range(1, stack_count):
        weight = jnp.where(pick_of_col == layer, weights[layer], weight)
    return weight


def orthonormal_coefficients(back, weight_gram):
    back_gram = product(back.T, product(weight_gram, back))
    lower = jnp.linalg.cholesky(back_gram)
    return lax.linalg.triangular_solve(lower, back, left_side=False, lower=True, transpose_a=True)


def on_device(latents, weights, start_basis, layer_pick):
    act = latents[0]
    weight = chosen_weight(weights, layer_pick)
    gram = jnp.dot(act.T, act, preferred_element_type=jnp.float32)
    weight_gram = jnp.dot(weight, weight.T, preferred_element_type=jnp.float32)
    image = jnp.dot(weight, start_basis, preferred_element_type=jnp.float32)
    gram, weight_gram, image = lax.psum((gram, weight_gram, image), ("tok", "head"))
    gram = gram / jnp.mean(jnp.diag(gram))
    image = image / jnp.sqrt(jnp.mean(image * image))
    for step in range(STEPS):
        coefficients = orthonormal_coefficients(product(gram, image), weight_gram)
        image = product(weight_gram, coefficients)
    scaled = coefficients * math.sqrt(OUT)
    high = lax.reduce_precision(scaled, 8, 7)
    low = scaled - high
    pieces = jnp.concatenate([high.astype(jnp.bfloat16), low.astype(jnp.bfloat16)], 1)
    both = jnp.dot(weight.T, pieces, preferred_element_type=jnp.float32)
    rank = scaled.shape[1]
    return ((both[:, :rank] + both[:, rank:])[None], image[None])


def solution(mesh):
    return jax.shard_map(
        on_device,
        mesh=mesh,
        in_specs=(
            P(("groups", "col"), ("tok", "head"), None),
            P(None, None, ("tok", "head")),
            P(("tok", "head"), None),
            P("groups", None),
        ),
        out_specs=(P(("groups", "col"), ("tok", "head"), None), P(("groups", "col"), None, None)),
        check_vma=False,
    )
```

```python
import functools
import math

import jax
import jax.numpy as jnp
from jax import lax
from jax.experimental import pallas as pl
from jax.experimental.pallas import tpu as pltpu
from jax.sharding import PartitionSpec as P

OUT = 32768
STEPS = 2
HEAD_OUT = 256
HALF = 256
PANEL = 8
BLOCK = 128
MESH = pl.DeviceIdType.MESH


def pack(packed, gram, first, diagonal):
    row = lax.broadcasted_iota(jnp.int32, (HALF, HALF), 0)
    column = lax.broadcasted_iota(jnp.int32, (HALF, HALF), 1)
    packed[first:first + HALF, :] = gram[:HALF, HALF:]
    bottom = gram[HALF:, HALF:]
    packed[first + HALF:first + 2 * HALF, :] = jnp.where(row >= column, gram[:HALF, :HALF], bottom)
    packed[diagonal:diagonal + 1, :] = jnp.sum(jnp.where(row == column, bottom, 0.0), axis=0, keepdims=True)


def local_sums_kernel(together, picks, act, start, *refs):
    weights, (packed, gram, weight_gram) = refs[:together], refs[together:]
    at = pl.program_id(0)
    width = gram.shape[0]

    @pl.when(at == 0)
    def _():
        packed[...] = jnp.zeros_like(packed)
        gram[...] = jnp.zeros_like(gram)
        weight_gram[...] = jnp.zeros_like(weight_gram)

    weight = jnp.concatenate([w[0] for w in weights], axis=1)
    gram[...] += lax.dot_general(act[...], act[...], (((0,), (0,)), ((), ())), preferred_element_type=jnp.float32)
    weight_gram[...] += lax.dot_general(weight, weight, (((1,), (1,)), ((), ())), preferred_element_type=jnp.float32)
    packed[:width, :] += jnp.dot(weight, start[...], preferred_element_type=jnp.float32)

    @pl.when(at == pl.num_programs(0) - 1)
    def _():
        pack(packed, gram, width, width + 4 * HALF)
        pack(packed, weight_gram, width + 2 * HALF, width + 4 * HALF + 1)


def weight_specs(together, width):
    def spec(k):
        return pl.BlockSpec((1, width, HEAD_OUT), lambda at, picks: (picks[at * together + k], 0, at * together + k))

    return [spec(k) for k in range(together)]


def local_sums(picks, act, start, weights, rows):
    width = act.shape[1]
    rank = start.shape[1]
    heads_here = picks.shape[0]
    together = math.gcd(heads_here, 4)
    steps = heads_here // together
    return pl.pallas_call(
        functools.partial(local_sums_kernel, together),
        out_shape=jax.ShapeDtypeStruct((rows, rank), jnp.float32),
        grid_spec=pltpu.PrefetchScalarGridSpec(
            num_scalar_prefetch=1,
            grid=(steps,),
            in_specs=[
                pl.BlockSpec((act.shape[0] // steps, width), lambda at, picks: (at, 0)),
                pl.BlockSpec((start.shape[0] // steps, rank), lambda at, picks: (at, 0)),
            ] + weight_specs(together, width),
            out_specs=pl.BlockSpec((rows, rank), lambda at, picks: (0, 0)),
            scratch_shapes=[pltpu.VMEM((width, width), jnp.float32)] * 2,
        ),
        compiler_params=pltpu.CompilerParams(vmem_limit_bytes=48 * 2**20),
        name="local_sums",
    )(picks, act, start, *[weights] * together)


def sum_kernel(count, x, out, from_core, chip_sum, from_chips, sems):
    me = lax.axis_index("tok")
    core = lax.axis_index("head")
    half = x.shape[0] // 2
    shard = half // count
    mine = core * half
    theirs = (1 - core) * half
    partner = {"head": 1 - core}

    def remote(source, target, stage, slot, device):
        return pltpu.make_async_remote_copy(
            src_ref=source, dst_ref=target, send_sem=sems.at[stage, 0, slot], recv_sem=sems.at[stage, 1, slot],
            device_id=device, device_id_type=MESH)

    def rows_of(base, index):
        return pl.ds(pl.multiple_of(base + index * shard, 8), shard)

    peers = [lax.rem(me + d, count) for d in range(count)]
    barrier = pltpu.get_barrier_semaphore()
    pl.semaphore_signal(barrier, inc=1, device_id=partner, device_id_type=MESH)
    for d in range(1, count):
        pl.semaphore_signal(barrier, inc=1, device_id={"tok": peers[d]}, device_id_type=MESH)
    pl.semaphore_wait(barrier, count)

    order = list(range(1, count)) + [0]
    first = [remote(x.at[rows_of(theirs, peers[d])], from_core.at[d], 0, d, partner) for d in range(count)]
    for d in order:
        first[d].start()
    second = [None] + [remote(chip_sum.at[d], from_chips.at[d], 1, d, {"tok": peers[d]}) for d in range(1, count)]
    for d in order:
        first[d].wait_recv()
        chip_sum[d] = x[rows_of(mine, peers[d]), :] + from_core[d]
        if d:
            second[d].start()
    total = chip_sum[0]
    for d in range(1, count):
        second[d].wait_recv()
        total = total + from_chips[d]
    own = rows_of(mine, me)
    out[own, :] = total
    third = [remote(out.at[own], out.at[own], 2, d, {"tok": peers[d]} if d else partner) for d in range(count)]
    for d in order:
        third[d].start()
    fourth = [None]
    for d in range(1, count):
        third[d].wait_recv()
        source = out.at[rows_of(mine, lax.rem(me - d + count, count))]
        fourth.append(remote(source, source, 3, d, partner))
        fourth[d].start()
    third[0].wait_recv()
    for d in range(1, count):
        fourth[d].wait_recv()
    for d in range(count):
        first[d].wait_send()
        third[d].wait_send()
        if d:
            second[d].wait_send()
            fourth[d].wait_send()


def summed(x):
    count = lax.axis_size("tok")
    shard = x.shape[0] // 2 // count
    slots = pltpu.VMEM((count, shard, x.shape[1]), jnp.float32)
    return pl.pallas_call(
        functools.partial(sum_kernel, count),
        out_shape=jax.ShapeDtypeStruct(x.shape, jnp.float32),
        in_specs=[pl.BlockSpec(memory_space=pltpu.VMEM)],
        out_specs=pl.BlockSpec(memory_space=pltpu.VMEM),
        scratch_shapes=[slots, slots, slots, pltpu.SemaphoreType.DMA((4, 2, count))],
        compiler_params=pltpu.CompilerParams(collective_id=0, has_side_effects=True, vmem_limit_bytes=48 * 2**20),
        name="summed",
    )(x)


def exact_dot(left, right, contract=(1, 0)):
    dims = (((contract[0],), (contract[1],)), ((), ()))
    return lax.dot_general(left, right, dims, precision=lax.Precision.HIGHEST, preferred_element_type=jnp.float32)


def inverse_factor(work, size):
    sublane = lax.broadcasted_iota(jnp.int32, (PANEL, 2 * size), 0)
    for first in range(0, size, PANEL):
        rows = work[first:first + PANEL, :]
        columns = [jnp.broadcast_to(rows[:, first + c:first + c + 1], (PANEL, 128)) for c in range(PANEL)]
        scale = jnp.zeros((PANEL, 128), jnp.float32)
        for c in range(PANEL):
            pivot = jnp.broadcast_to(columns[c][c:c + 1, :], (PANEL, 128))
            scale = jnp.where(sublane[:, :128] == c, pivot, scale)
            if c == PANEL - 1:
                break
            factor = jnp.where(sublane[:, :128] > c, columns[c] / pivot, 0.0)
            for later in range(c + 1, PANEL):
                columns[later] = columns[later] - factor * columns[later][c:c + 1, :]
            wide = jnp.concatenate([factor] * (2 * size // 128), axis=1)
            rows = rows - wide * rows[c:c + 1, :]
        inverse_root = lax.rsqrt(scale)
        rows = rows * jnp.concatenate([inverse_root] * (2 * size // 128), axis=1)
        work[first:first + PANEL, :] = rows
        rest = first + PANEL
        if rest < size:
            update = exact_dot(rows[:, :size], rows, (0, 0))
            work[rest:, :] = work[rest:, :] - update[rest:, :]
    return work[:, size:]


def unpacked(packed, first, diagonal):
    corner = packed[first:first + HALF, :]
    triangles = packed[first + HALF:first + 2 * HALF, :]
    row = lax.broadcasted_iota(jnp.int32, (HALF, HALF), 0)
    column = lax.broadcasted_iota(jnp.int32, (HALF, HALF), 1)
    flipped = triangles.T
    top = jnp.where(row >= column, triangles, flipped)
    bottom = jnp.where(row < column, triangles, flipped)
    bottom = jnp.where(row == column, jnp.broadcast_to(packed[diagonal:diagonal + 1, :], (HALF, HALF)), bottom)
    return jnp.concatenate([
        jnp.concatenate([top, corner], axis=1),
        jnp.concatenate([corner.T, bottom], axis=1),
    ], axis=0)


def chain_kernel(packed, image_out, pieces_out, weight_gram_ref, image_work, back_work, work):
    width, rank = image_work.shape
    row = lax.broadcasted_iota(jnp.int32, (width, width), 0)
    column = lax.broadcasted_iota(jnp.int32, (width, width), 1)
    gram = unpacked(packed, width, width + 4 * HALF)
    gram = gram / (jnp.sum(jnp.where(row == column, gram, 0.0)) / width)
    weight_gram_ref[...] = unpacked(packed, width + 2 * HALF, width + 4 * HALF + 1)
    image = packed[:width, :]
    image_work[...] = image / jnp.sqrt(jnp.mean(image * image))
    eye = (row[:BLOCK, :BLOCK] == column[:BLOCK, :BLOCK]).astype(jnp.float32)

    def step(_, carry):
        back = exact_dot(gram, image_work[...])
        mixed = exact_dot(weight_gram_ref[...], back)
        square = exact_dot(back, mixed, (0, 0))
        pieces = []
        count = rank // BLOCK
        schur = {}
        for i in range(count):
            for j in range(i + 1):
                schur[i, j] = square[i * BLOCK:(i + 1) * BLOCK, j * BLOCK:(j + 1) * BLOCK]
        inverse = []
        below = {}
        done = []
        for i in range(count):
            current = schur[i, i]
            work[:, :BLOCK] = current
            work[:, BLOCK:] = eye
            inv = inverse_factor(work, BLOCK)
            lower_mask = row[:BLOCK, :BLOCK] >= column[:BLOCK, :BLOCK]
            inv = jnp.where(lower_mask, inv, 0.0)
            part_back = back[:, i * BLOCK:(i + 1) * BLOCK]
            part_mixed = mixed[:, i * BLOCK:(i + 1) * BLOCK]
            for j in range(i):
                part_back = part_back - exact_dot(done[j][0], below[i, j], (1, 1))
                part_mixed = part_mixed - exact_dot(done[j][1], below[i, j], (1, 1))
            part_back = exact_dot(part_back, inv, (1, 1))
            part_mixed = exact_dot(part_mixed, inv, (1, 1))
            done.append((part_back, part_mixed))
            for k in range(i + 1, count):
                below[k, i] = exact_dot(schur[k, i], inv, (1, 1))
            for k in range(i + 1, count):
                for m in range(i + 1, k + 1):
                    schur[k, m] = schur[k, m] - exact_dot(below[k, i], below[m, i], (1, 1))
        back_work[...] = jnp.concatenate([d[0] for d in done], axis=1)
        image_work[...] = jnp.concatenate([d[1] for d in done], axis=1)
        return carry

    lax.fori_loop(0, STEPS, step, 0)
    image_out[...] = image_work[...]
    scaled = back_work[...] * math.sqrt(OUT)
    high = scaled.astype(jnp.bfloat16)
    pieces_out[:, :rank] = high
    pieces_out[:, rank:] = (scaled - high.astype(jnp.float32)).astype(jnp.bfloat16)


def chain(packed, width, rank):
    return pl.pallas_call(
        chain_kernel,
        out_shape=(jax.ShapeDtypeStruct((width, rank), jnp.float32), jax.ShapeDtypeStruct((width, 2 * rank), jnp.bfloat16)),
        in_specs=[pl.BlockSpec(memory_space=pltpu.VMEM)],
        out_specs=(pl.BlockSpec(memory_space=pltpu.VMEM),) * 2,
        scratch_shapes=[
            pltpu.VMEM((width, width), jnp.float32),
            pltpu.VMEM((width, rank), jnp.float32),
            pltpu.VMEM((width, rank), jnp.float32),
            pltpu.VMEM((BLOCK, 2 * BLOCK), jnp.float32),
        ],
        compiler_params=pltpu.CompilerParams(vmem_limit_bytes=48 * 2**20),
        name="chain",
    )(packed)


def basis_kernel(together, picks, pieces, *refs):
    weights, out = refs[:together], refs[together]
    rank = out.shape[1]
    for k, weight in enumerate(weights):
        both = lax.dot_general(weight[0], pieces[...], (((0,), (0,)), ((), ())), preferred_element_type=jnp.float32)
        out[k * HEAD_OUT:(k + 1) * HEAD_OUT, :] = both[:, :rank] + both[:, rank:]


def back_projected(picks, pieces, weights):
    width = pieces.shape[0]
    rank = pieces.shape[1] // 2
    heads_here = picks.shape[0]
    together = math.gcd(heads_here, 4)
    return pl.pallas_call(
        functools.partial(basis_kernel, together),
        out_shape=jax.ShapeDtypeStruct((heads_here * HEAD_OUT, rank), jnp.float32),
        grid_spec=pltpu.PrefetchScalarGridSpec(
            num_scalar_prefetch=1,
            grid=(heads_here // together,),
            in_specs=[pl.BlockSpec(pieces.shape, lambda at, picks: (0, 0))] + weight_specs(together, width),
            out_specs=pl.BlockSpec((together * HEAD_OUT, rank), lambda at, picks: (at, 0)),
        ),
        compiler_params=pltpu.CompilerParams(vmem_limit_bytes=48 * 2**20),
        name="back_projected",
    )(picks, pieces, *[weights] * together)


def on_device(latents, weights, start_basis, layer_pick):
    act = latents[0]
    width = act.shape[1]
    rank = start_basis.shape[1]
    heads_here = weights.shape[2] // HEAD_OUT
    slot = lax.axis_index("col")
    first_head = lax.axis_index(("tok", "head")) * heads_here
    picks = lax.dynamic_slice(layer_pick, (slot, first_head), (1, heads_here))[0]
    unit = 16 * lax.axis_size("tok")
    rows = -(-(width + 4 * HALF + 2) // unit) * unit
    packed = summed(local_sums(picks, act, start_basis, weights, rows))
    core, pieces = chain(packed, width, rank)
    return (back_projected(picks, pieces, weights)[None], core[None])


def solution(mesh):
    return jax.shard_map(
        on_device,
        mesh=mesh,
        in_specs=(
            P(("groups", "col"), ("tok", "head"), None),
            P(None, None, ("tok", "head")),
            P(("tok", "head"), None),
            P("groups", None),
        ),
        out_specs=(P(("groups", "col"), ("tok", "head"), None), P(("groups", "col"), None, None)),
        check_vma=False,
    )
```

```python
import functools
import math

import jax
import jax.numpy as jnp
from jax import lax
from jax.experimental import pallas as pl
from jax.experimental.pallas import tpu as pltpu
from jax.sharding import PartitionSpec as P

OUT = 32768
STEPS = 2
HEAD_OUT = 256
HALF = 256
PANEL = 8
BLOCK = 128
CHUNKS = 10
MESH = pl.DeviceIdType.MESH


def pack(packed, gram, first, diagonal):
    row = lax.broadcasted_iota(jnp.int32, (HALF, HALF), 0)
    column = lax.broadcasted_iota(jnp.int32, (HALF, HALF), 1)
    packed[first:first + HALF, :] = gram[:HALF, HALF:]
    bottom = gram[HALF:, HALF:]
    packed[first + HALF:first + 2 * HALF, :] = jnp.where(row >= column, gram[:HALF, :HALF], bottom)
    packed[diagonal:diagonal + 1, :] = jnp.sum(jnp.where(row == column, bottom, 0.0), axis=0, keepdims=True)


def local_sums_kernel(together, picks, act, start, *refs):
    weights, (packed, gram, weight_gram) = refs[:together], refs[together:]
    at = pl.program_id(0)
    width = gram.shape[0]

    @pl.when(at == 0)
    def _():
        packed[...] = jnp.zeros_like(packed)
        gram[...] = jnp.zeros_like(gram)
        weight_gram[...] = jnp.zeros_like(weight_gram)

    weight = jnp.concatenate([w[0] for w in weights], axis=1)
    gram[...] += lax.dot_general(act[...], act[...], (((0,), (0,)), ((), ())), preferred_element_type=jnp.float32)
    weight_gram[...] += lax.dot_general(weight, weight, (((1,), (1,)), ((), ())), preferred_element_type=jnp.float32)
    packed[:width, :] += jnp.dot(weight, start[...], preferred_element_type=jnp.float32)

    @pl.when(at == pl.num_programs(0) - 1)
    def _():
        pack(packed, gram, width, width + 4 * HALF)
        pack(packed, weight_gram, width + 2 * HALF, width + 4 * HALF + 1)


def weight_specs(together, width):
    def spec(k):
        return pl.BlockSpec((1, width, HEAD_OUT), lambda at, picks: (picks[at * together + k], 0, at * together + k))

    return [spec(k) for k in range(together)]


def local_sums(picks, act, start, weights, rows):
    width = act.shape[1]
    rank = start.shape[1]
    heads_here = picks.shape[0]
    together = math.gcd(heads_here, 4)
    steps = heads_here // together
    return pl.pallas_call(
        functools.partial(local_sums_kernel, together),
        out_shape=jax.ShapeDtypeStruct((rows, rank), jnp.float32),
        grid_spec=pltpu.PrefetchScalarGridSpec(
            num_scalar_prefetch=1,
            grid=(steps,),
            in_specs=[
                pl.BlockSpec((act.shape[0] // steps, width), lambda at, picks: (at, 0)),
                pl.BlockSpec((start.shape[0] // steps, rank), lambda at, picks: (at, 0)),
            ] + weight_specs(together, width),
            out_specs=pl.BlockSpec((rows, rank), lambda at, picks: (0, 0)),
            scratch_shapes=[pltpu.VMEM((width, width), jnp.float32)] * 2,
        ),
        compiler_params=pltpu.CompilerParams(vmem_limit_bytes=48 * 2**20),
        name="local_sums",
    )(picks, act, start, *[weights] * together)


def sum_kernel(count, x, out, from_core, chip_sum, from_back, sems):
    me = lax.axis_index("tok")
    core = lax.axis_index("head")
    half = x.shape[0] // 2
    chunk = half // CHUNKS
    mine = core * half
    theirs = (1 - core) * half
    partner = {"head": 1 - core}
    place = jnp.where(core == 0, me, count - 1 - me)
    ahead = {"tok": jnp.where(core == 0, me + 1, me - 1)}
    behind = {"tok": jnp.where(core == 0, me - 1, me + 1)}
    is_first = place == 0
    is_last = place == count - 1

    def remote(source, target, stage, k, device):
        return pltpu.make_async_remote_copy(
            src_ref=source, dst_ref=target, send_sem=sems.at[stage, 0, k], recv_sem=sems.at[stage, 1, k],
            device_id=device, device_id_type=MESH)

    def rows_of(base, k):
        return pl.ds(pl.multiple_of(base + k * chunk, 8), chunk)

    def to_core(k):
        return remote(x.at[rows_of(theirs, k)], from_core.at[k], 0, k, partner)

    def onward(k):
        return remote(chip_sum.at[k], from_back.at[k], 1, k, ahead)

    def returned(k):
        rows = rows_of(mine, k)
        return remote(out.at[rows], out.at[rows], 2, k, behind)

    def shared(k):
        rows = rows_of(mine, k)
        return remote(out.at[rows], out.at[rows], 3, k, partner)

    barrier = pltpu.get_barrier_semaphore()
    pl.semaphore_signal(barrier, inc=1, device_id=partner, device_id_type=MESH)

    @pl.when(jnp.logical_not(is_first))
    def _():
        pl.semaphore_signal(barrier, inc=1, device_id=behind, device_id_type=MESH)

    @pl.when(jnp.logical_not(is_last))
    def _():
        pl.semaphore_signal(barrier, inc=1, device_id=ahead, device_id_type=MESH)

    at_end = jnp.logical_or(is_first, is_last)

    @pl.when(at_end)
    def _():
        pl.semaphore_wait(barrier, 2)

    @pl.when(jnp.logical_not(at_end))
    def _():
        pl.semaphore_wait(barrier, 3)

    def start(k, carry):
        to_core(k).start()
        return carry

    lax.fori_loop(0, CHUNKS, start, 0)
    lag = 2 * (count - 1 - place)

    def body(i, carry):
        @pl.when(i < CHUNKS)
        def _():
            to_core(i).wait_recv()
            chip_sum[i] = x[rows_of(mine, i), :] + from_core[i]

            @pl.when(jnp.logical_not(is_first))
            def _():
                onward(i).wait_recv()
                chip_sum[i] = chip_sum[i] + from_back[i]

            @pl.when(jnp.logical_not(is_last))
            def _():
                onward(i).start()

            @pl.when(is_last)
            def _():
                out[rows_of(mine, i), :] = chip_sum[i]

        k = i - lag

        @pl.when(jnp.logical_and(k >= 0, k < CHUNKS))
        def _():
            @pl.when(jnp.logical_not(is_last))
            def _():
                returned(k).wait_recv()

            @pl.when(jnp.logical_not(is_first))
            def _():
                returned(k).start()

            shared(k).start()

        return carry

    lax.fori_loop(0, CHUNKS + 2 * (count - 1), body, 0)

    def finish(k, carry):
        shared(k).wait_recv()
        shared(k).wait_send()
        to_core(k).wait_send()

        @pl.when(jnp.logical_not(is_last))
        def _():
            onward(k).wait_send()

        @pl.when(jnp.logical_not(is_first))
        def _():
            returned(k).wait_send()

        return carry

    lax.fori_loop(0, CHUNKS, finish, 0)


def summed(x):
    count = lax.axis_size("tok")
    chunk = x.shape[0] // 2 // CHUNKS
    slots = pltpu.VMEM((CHUNKS, chunk, x.shape[1]), jnp.float32)
    return pl.pallas_call(
        functools.partial(sum_kernel, count),
        out_shape=jax.ShapeDtypeStruct(x.shape, jnp.float32),
        in_specs=[pl.BlockSpec(memory_space=pltpu.VMEM)],
        out_specs=pl.BlockSpec(memory_space=pltpu.VMEM),
        scratch_shapes=[slots, slots, slots, pltpu.SemaphoreType.DMA((4, 2, CHUNKS))],
        compiler_params=pltpu.CompilerParams(collective_id=0, has_side_effects=True, vmem_limit_bytes=48 * 2**20),
        name="summed",
    )(x)


def exact_dot(left, right, contract=(1, 0)):
    dims = (((contract[0],), (contract[1],)), ((), ()))
    return lax.dot_general(left, right, dims, precision=lax.Precision.HIGHEST, preferred_element_type=jnp.float32)


def stacked_dot(rows, size):
    high = rows.astype(jnp.bfloat16).astype(jnp.float32)
    rest = rows - high
    middle = rest.astype(jnp.bfloat16).astype(jnp.float32)
    low = rest - middle
    left = jnp.concatenate([p[:, :size] for p in (high, high, middle, high, low, middle)], axis=0).astype(jnp.bfloat16)
    right = jnp.concatenate([high, middle, high, low, high, middle], axis=0).astype(jnp.bfloat16)
    return lax.dot_general(left, right, (((0,), (0,)), ((), ())), preferred_element_type=jnp.float32)


def inverse_factor(work, size):
    sublane = lax.broadcasted_iota(jnp.int32, (PANEL, 2 * size), 0)
    for first in range(0, size, PANEL):
        rows = work[first:first + PANEL, :]
        columns = [jnp.broadcast_to(rows[:, first + c:first + c + 1], (PANEL, 128)) for c in range(PANEL)]
        scale = jnp.zeros((PANEL, 128), jnp.float32)
        for c in range(PANEL):
            pivot = jnp.broadcast_to(columns[c][c:c + 1, :], (PANEL, 128))
            scale = jnp.where(sublane[:, :128] == c, pivot, scale)
            if c == PANEL - 1:
                break
            factor = jnp.where(sublane[:, :128] > c, columns[c] / pivot, 0.0)
            for later in range(c + 1, PANEL):
                columns[later] = columns[later] - factor * columns[later][c:c + 1, :]
            wide = jnp.concatenate([factor] * (2 * size // 128), axis=1)
            rows = rows - wide * rows[c:c + 1, :]
        inverse_root = lax.rsqrt(scale)
        rows = rows * jnp.concatenate([inverse_root] * (2 * size // 128), axis=1)
        work[first:first + PANEL, :] = rows
        rest = first + PANEL
        if rest < size:
            update = stacked_dot(rows, size)
            work[rest:, :] = work[rest:, :] - update[rest:, :]
    return work[:, size:]


def unpacked(packed, first, diagonal):
    corner = packed[first:first + HALF, :]
    triangles = packed[first + HALF:first + 2 * HALF, :]
    row = lax.broadcasted_iota(jnp.int32, (HALF, HALF), 0)
    column = lax.broadcasted_iota(jnp.int32, (HALF, HALF), 1)
    flipped = triangles.T
    top = jnp.where(row >= column, triangles, flipped)
    bottom = jnp.where(row < column, triangles, flipped)
    bottom = jnp.where(row == column, jnp.broadcast_to(packed[diagonal:diagonal + 1, :], (HALF, HALF)), bottom)
    return jnp.concatenate([
        jnp.concatenate([top, corner], axis=1),
        jnp.concatenate([corner.T, bottom], axis=1),
    ], axis=0)


def chain_kernel(packed, image_out, pieces_out, weight_gram_ref, image_work, back_work, work):
    width, rank = image_work.shape
    row = lax.broadcasted_iota(jnp.int32, (width, width), 0)
    column = lax.broadcasted_iota(jnp.int32, (width, width), 1)
    gram = unpacked(packed, width, width + 4 * HALF)
    gram = gram / (jnp.sum(jnp.where(row == column, gram, 0.0)) / width)
    weight_gram_ref[...] = unpacked(packed, width + 2 * HALF, width + 4 * HALF + 1)
    image = packed[:width, :]
    image_work[...] = image / jnp.sqrt(jnp.mean(image * image))
    eye = (row[:BLOCK, :BLOCK] == column[:BLOCK, :BLOCK]).astype(jnp.float32)

    def step(_, carry):
        back = exact_dot(gram, image_work[...])
        mixed = exact_dot(weight_gram_ref[...], back)
        square = exact_dot(back, mixed, (0, 0))
        pieces = []
        count = rank // BLOCK
        schur = {}
        for i in range(count):
            for j in range(i + 1):
                schur[i, j] = square[i * BLOCK:(i + 1) * BLOCK, j * BLOCK:(j + 1) * BLOCK]
        inverse = []
        below = {}
        done = []
        for i in range(count):
            current = schur[i, i]
            work[:, :BLOCK] = current
            work[:, BLOCK:] = eye
            inv = inverse_factor(work, BLOCK)
            lower_mask = row[:BLOCK, :BLOCK] >= column[:BLOCK, :BLOCK]
            inv = jnp.where(lower_mask, inv, 0.0)
            part_back = back[:, i * BLOCK:(i + 1) * BLOCK]
            part_mixed = mixed[:, i * BLOCK:(i + 1) * BLOCK]
            for j in range(i):
                part_back = part_back - exact_dot(done[j][0], below[i, j], (1, 1))
                part_mixed = part_mixed - exact_dot(done[j][1], below[i, j], (1, 1))
            part_back = exact_dot(part_back, inv, (1, 1))
            part_mixed = exact_dot(part_mixed, inv, (1, 1))
            done.append((part_back, part_mixed))
            for k in range(i + 1, count):
                below[k, i] = exact_dot(schur[k, i], inv, (1, 1))
            for k in range(i + 1, count):
                for m in range(i + 1, k + 1):
                    schur[k, m] = schur[k, m] - exact_dot(below[k, i], below[m, i], (1, 1))
        back_work[...] = jnp.concatenate([d[0] for d in done], axis=1)
        image_work[...] = jnp.concatenate([d[1] for d in done], axis=1)
        return carry

    lax.fori_loop(0, STEPS, step, 0)
    image_out[...] = image_work[...]
    scaled = back_work[...] * math.sqrt(OUT)
    high = scaled.astype(jnp.bfloat16)
    pieces_out[:, :rank] = high
    pieces_out[:, rank:] = (scaled - high.astype(jnp.float32)).astype(jnp.bfloat16)


def chain(packed, width, rank):
    return pl.pallas_call(
        chain_kernel,
        out_shape=(jax.ShapeDtypeStruct((width, rank), jnp.float32), jax.ShapeDtypeStruct((width, 2 * rank), jnp.bfloat16)),
        in_specs=[pl.BlockSpec(memory_space=pltpu.VMEM)],
        out_specs=(pl.BlockSpec(memory_space=pltpu.VMEM),) * 2,
        scratch_shapes=[
            pltpu.VMEM((width, width), jnp.float32),
            pltpu.VMEM((width, rank), jnp.float32),
            pltpu.VMEM((width, rank), jnp.float32),
            pltpu.VMEM((BLOCK, 2 * BLOCK), jnp.float32),
        ],
        compiler_params=pltpu.CompilerParams(vmem_limit_bytes=48 * 2**20),
        name="chain",
    )(packed)


def basis_kernel(together, picks, pieces, *refs):
    weights, out = refs[:together], refs[together]
    rank = out.shape[1]
    for k, weight in enumerate(weights):
        both = lax.dot_general(weight[0], pieces[...], (((0,), (0,)), ((), ())), preferred_element_type=jnp.float32)
        out[k * HEAD_OUT:(k + 1) * HEAD_OUT, :] = both[:, :rank] + both[:, rank:]


def back_projected(picks, pieces, weights):
    width = pieces.shape[0]
    rank = pieces.shape[1] // 2
    heads_here = picks.shape[0]
    together = math.gcd(heads_here, 4)
    return pl.pallas_call(
        functools.partial(basis_kernel, together),
        out_shape=jax.ShapeDtypeStruct((heads_here * HEAD_OUT, rank), jnp.float32),
        grid_spec=pltpu.PrefetchScalarGridSpec(
            num_scalar_prefetch=1,
            grid=(heads_here // together,),
            in_specs=[pl.BlockSpec(pieces.shape, lambda at, picks: (0, 0))] + weight_specs(together, width),
            out_specs=pl.BlockSpec((together * HEAD_OUT, rank), lambda at, picks: (at, 0)),
        ),
        compiler_params=pltpu.CompilerParams(vmem_limit_bytes=48 * 2**20),
        name="back_projected",
    )(picks, pieces, *[weights] * together)


def on_device(latents, weights, start_basis, layer_pick):
    act = latents[0]
    width = act.shape[1]
    rank = start_basis.shape[1]
    heads_here = weights.shape[2] // HEAD_OUT
    slot = lax.axis_index("col")
    first_head = lax.axis_index(("tok", "head")) * heads_here
    picks = lax.dynamic_slice(layer_pick, (slot, first_head), (1, heads_here))[0]
    unit = 16 * CHUNKS
    rows = -(-(width + 4 * HALF + 2) // unit) * unit
    packed = summed(local_sums(picks, act, start_basis, weights, rows))
    core, pieces = chain(packed, width, rank)
    return (back_projected(picks, pieces, weights)[None], core[None])


def solution(mesh):
    return jax.shard_map(
        on_device,
        mesh=mesh,
        in_specs=(
            P(("groups", "col"), ("tok", "head"), None),
            P(None, None, ("tok", "head")),
            P(("tok", "head"), None),
            P("groups", None),
        ),
        out_specs=(P(("groups", "col"), ("tok", "head"), None), P(("groups", "col"), None, None)),
        check_vma=False,
    )
```

```python
import functools
import math

import jax
import jax.numpy as jnp
from jax import lax
from jax.experimental import pallas as pl
from jax.experimental.pallas import tpu as pltpu
from jax.sharding import PartitionSpec as P

OUT = 32768
STEPS = 2
HEAD_OUT = 256
HALF = 256
PANEL = 8
BLOCK = 128
MESH = pl.DeviceIdType.MESH


def pack(packed, gram, first, diagonal):
    row = lax.broadcasted_iota(jnp.int32, (HALF, HALF), 0)
    column = lax.broadcasted_iota(jnp.int32, (HALF, HALF), 1)
    packed[first:first + HALF, :] = gram[:HALF, HALF:]
    bottom = gram[HALF:, HALF:]
    packed[first + HALF:first + 2 * HALF, :] = jnp.where(row >= column, gram[:HALF, :HALF], bottom)
    packed[diagonal:diagonal + 1, :] = jnp.sum(jnp.where(row == column, bottom, 0.0), axis=0, keepdims=True)


def local_sums_kernel(together, picks, act, start, *refs):
    weights, (packed, gram, weight_gram) = refs[:together], refs[together:]
    at = pl.program_id(0)
    width = gram.shape[0]

    @pl.when(at == 0)
    def _():
        packed[...] = jnp.zeros_like(packed)
        gram[...] = jnp.zeros_like(gram)
        weight_gram[...] = jnp.zeros_like(weight_gram)

    weight = jnp.concatenate([w[0] for w in weights], axis=1)
    gram[...] += lax.dot_general(act[...], act[...], (((0,), (0,)), ((), ())), preferred_element_type=jnp.float32)
    weight_gram[...] += lax.dot_general(weight, weight, (((1,), (1,)), ((), ())), preferred_element_type=jnp.float32)
    packed[:width, :] += jnp.dot(weight, start[...], preferred_element_type=jnp.float32)

    @pl.when(at == pl.num_programs(0) - 1)
    def _():
        pack(packed, gram, width, width + 4 * HALF)
        pack(packed, weight_gram, width + 2 * HALF, width + 4 * HALF + 1)


def weight_specs(together, width):
    def spec(k):
        return pl.BlockSpec((1, width, HEAD_OUT), lambda at, picks: (picks[at * together + k], 0, at * together + k))

    return [spec(k) for k in range(together)]


def local_sums(picks, act, start, weights, rows):
    width = act.shape[1]
    rank = start.shape[1]
    heads_here = picks.shape[0]
    together = math.gcd(heads_here, 4)
    steps = heads_here // together
    return pl.pallas_call(
        functools.partial(local_sums_kernel, together),
        out_shape=jax.ShapeDtypeStruct((rows, rank), jnp.float32),
        grid_spec=pltpu.PrefetchScalarGridSpec(
            num_scalar_prefetch=1,
            grid=(steps,),
            in_specs=[
                pl.BlockSpec((act.shape[0] // steps, width), lambda at, picks: (at, 0)),
                pl.BlockSpec((start.shape[0] // steps, rank), lambda at, picks: (at, 0)),
            ] + weight_specs(together, width),
            out_specs=pl.BlockSpec((rows, rank), lambda at, picks: (0, 0)),
            scratch_shapes=[pltpu.VMEM((width, width), jnp.float32)] * 2,
        ),
        compiler_params=pltpu.CompilerParams(vmem_limit_bytes=48 * 2**20),
        name="local_sums",
    )(picks, act, start, *[weights] * together)


def sum_kernel(count, x, out, from_core, chip_sum, from_chips, sems):
    me = lax.axis_index("tok")
    core = lax.axis_index("head")
    half = x.shape[0] // 2
    shard = half // count
    mine = core * half
    theirs = (1 - core) * half
    partner = {"head": 1 - core}

    def remote(source, target, stage, slot, device):
        return pltpu.make_async_remote_copy(
            src_ref=source, dst_ref=target, send_sem=sems.at[stage, 0, slot], recv_sem=sems.at[stage, 1, slot],
            device_id=device, device_id_type=MESH)

    def rows_of(base, index):
        return pl.ds(pl.multiple_of(base + index * shard, 8), shard)

    peers = [lax.rem(me + d, count) for d in range(count)]
    barrier = pltpu.get_barrier_semaphore()
    pl.semaphore_signal(barrier, inc=1, device_id=partner, device_id_type=MESH)
    for d in range(1, count):
        pl.semaphore_signal(barrier, inc=1, device_id={"tok": peers[d]}, device_id_type=MESH)
    pl.semaphore_wait(barrier, count)

    order = list(range(1, count)) + [0]
    first = [remote(x.at[rows_of(theirs, peers[d])], from_core.at[d], 0, d, partner) for d in range(count)]
    for d in order:
        first[d].start()
    second = [None] + [remote(chip_sum.at[d], from_chips.at[d], 1, d, {"tok": peers[d]}) for d in range(1, count)]
    for d in order:
        first[d].wait_recv()
        chip_sum[d] = x[rows_of(mine, peers[d]), :] + from_core[d]
        if d:
            second[d].start()
    total = chip_sum[0]
    for d in range(1, count):
        second[d].wait_recv()
        total = total + from_chips[d]
    own = rows_of(mine, me)
    out[own, :] = total
    third = [remote(out.at[own], out.at[own], 2, d, {"tok": peers[d]} if d else partner) for d in range(count)]
    for d in order:
        third[d].start()
    fourth = [None]
    for d in range(1, count):
        third[d].wait_recv()
        source = out.at[rows_of(mine, lax.rem(me - d + count, count))]
        fourth.append(remote(source, source, 3, d, partner))
        fourth[d].start()
    third[0].wait_recv()
    for d in range(1, count):
        fourth[d].wait_recv()
    for d in range(count):
        first[d].wait_send()
        third[d].wait_send()
        if d:
            second[d].wait_send()
            fourth[d].wait_send()


def summed(x):
    count = lax.axis_size("tok")
    shard = x.shape[0] // 2 // count
    slots = pltpu.VMEM((count, shard, x.shape[1]), jnp.float32)
    return pl.pallas_call(
        functools.partial(sum_kernel, count),
        out_shape=jax.ShapeDtypeStruct(x.shape, jnp.float32),
        in_specs=[pl.BlockSpec(memory_space=pltpu.VMEM)],
        out_specs=pl.BlockSpec(memory_space=pltpu.VMEM),
        scratch_shapes=[slots, slots, slots, pltpu.SemaphoreType.DMA((4, 2, count))],
        compiler_params=pltpu.CompilerParams(collective_id=0, has_side_effects=True, vmem_limit_bytes=48 * 2**20),
        name="summed",
    )(x)


def exact_dot(left, right, contract=(1, 0)):
    dims = (((contract[0],), (contract[1],)), ((), ()))
    return lax.dot_general(left, right, dims, precision=lax.Precision.HIGHEST, preferred_element_type=jnp.float32)


def stacked_dot(rows, size):
    high = rows.astype(jnp.bfloat16).astype(jnp.float32)
    rest = rows - high
    middle = rest.astype(jnp.bfloat16).astype(jnp.float32)
    low = rest - middle
    left = jnp.concatenate([p[:, :size] for p in (high, high, middle, high, low, middle)], axis=0).astype(jnp.bfloat16)
    right = jnp.concatenate([high, middle, high, low, high, middle], axis=0).astype(jnp.bfloat16)
    return lax.dot_general(left, right, (((0,), (0,)), ((), ())), preferred_element_type=jnp.float32)


def eliminate_panel(work, size, first):
    sublane = lax.broadcasted_iota(jnp.int32, (PANEL, 128), 0)
    rows = work[first:first + PANEL, :]
    columns = [jnp.broadcast_to(rows[:, first + c:first + c + 1], (PANEL, 128)) for c in range(PANEL)]
    scale = jnp.zeros((PANEL, 128), jnp.float32)
    for c in range(PANEL):
        pivot = jnp.broadcast_to(columns[c][c:c + 1, :], (PANEL, 128))
        scale = jnp.where(sublane == c, pivot, scale)
        if c == PANEL - 1:
            break
        factor = jnp.where(sublane > c, columns[c] / pivot, 0.0)
        for later in range(c + 1, PANEL):
            columns[later] = columns[later] - factor * columns[later][c:c + 1, :]
        wide = jnp.concatenate([factor] * (2 * size // 128), axis=1)
        rows = rows - wide * rows[c:c + 1, :]
    inverse_root = lax.rsqrt(scale)
    rows = rows * jnp.concatenate([inverse_root] * (2 * size // 128), axis=1)
    work[first:first + PANEL, :] = rows
    rest = first + PANEL
    if rest < size:
        work[rest:, :] = work[rest:, :] - stacked_dot(rows, size)[rest:, :]


def inverse_factors(works, blocks):
    size = blocks[0].shape[0]
    row = lax.broadcasted_iota(jnp.int32, (size, size), 0)
    column = lax.broadcasted_iota(jnp.int32, (size, size), 1)
    for work, block in zip(works, blocks):
        work[:, :size] = block
        work[:, size:] = (row == column).astype(jnp.float32)
    for first in range(0, size, PANEL):
        for work, _ in zip(works, blocks):
            eliminate_panel(work, size, first)
    return [jnp.where(row >= column, work[:, size:], 0.0) for work, _ in zip(works, blocks)]


def unpacked(packed, first, diagonal):
    corner = packed[first:first + HALF, :]
    triangles = packed[first + HALF:first + 2 * HALF, :]
    row = lax.broadcasted_iota(jnp.int32, (HALF, HALF), 0)
    column = lax.broadcasted_iota(jnp.int32, (HALF, HALF), 1)
    flipped = triangles.T
    top = jnp.where(row >= column, triangles, flipped)
    bottom = jnp.where(row < column, triangles, flipped)
    bottom = jnp.where(row == column, jnp.broadcast_to(packed[diagonal:diagonal + 1, :], (HALF, HALF)), bottom)
    return jnp.concatenate([
        jnp.concatenate([top, corner], axis=1),
        jnp.concatenate([corner.T, bottom], axis=1),
    ], axis=0)


def blocks_of(square):
    count = square.shape[0] // BLOCK
    return {(i, j): square[i * BLOCK:(i + 1) * BLOCK, j * BLOCK:(j + 1) * BLOCK] for i in range(count) for j in range(i + 1)}


def conditioned(works, back, mixed, square):
    blocks = blocks_of(square)
    count = square.shape[0] // BLOCK
    inverses = inverse_factors(works, [blocks[i, i] for i in range(count)])
    done = []
    for i, inverse in enumerate(inverses):
        here = slice(i * BLOCK, (i + 1) * BLOCK)
        part_back = exact_dot(back[:, here], inverse, (1, 1))
        part_mixed = exact_dot(mixed[:, here], inverse, (1, 1))
        for before_back, before_mixed in done:
            shared = exact_dot(before_back, part_mixed, (0, 0))
            part_back = part_back - exact_dot(before_back, shared)
            part_mixed = part_mixed - exact_dot(before_mixed, shared)
        done.append((part_back, part_mixed))
    return done


def orthonormal(works, back, mixed, square):
    schur = blocks_of(square)
    count = square.shape[0] // BLOCK
    below = {}
    done = []
    for i in range(count):
        here = slice(i * BLOCK, (i + 1) * BLOCK)
        inverse, = inverse_factors(works[:1], [schur[i, i]])
        part_back = back[:, here]
        part_mixed = mixed[:, here]
        for j in range(i):
            part_back = part_back - exact_dot(done[j][0], below[i, j], (1, 1))
            part_mixed = part_mixed - exact_dot(done[j][1], below[i, j], (1, 1))
        done.append((exact_dot(part_back, inverse, (1, 1)), exact_dot(part_mixed, inverse, (1, 1))))
        for k in range(i + 1, count):
            below[k, i] = exact_dot(schur[k, i], inverse, (1, 1))
        for k in range(i + 1, count):
            for m in range(i + 1, k + 1):
                schur[k, m] = schur[k, m] - exact_dot(below[k, i], below[m, i], (1, 1))
    return done


def chain_kernel(packed, image_out, pieces_out, weight_gram_ref, image_work, back_work, *works):
    width, rank = image_work.shape
    row = lax.broadcasted_iota(jnp.int32, (width, width), 0)
    column = lax.broadcasted_iota(jnp.int32, (width, width), 1)
    gram = unpacked(packed, width, width + 4 * HALF)
    gram = gram / (jnp.sum(jnp.where(row == column, gram, 0.0)) / width)
    weight_gram_ref[...] = unpacked(packed, width + 2 * HALF, width + 4 * HALF + 1)
    image = packed[:width, :]
    image_work[...] = image / jnp.sqrt(jnp.mean(image * image))
    for step in range(STEPS):
        back = exact_dot(gram, image_work[...])
        mixed = exact_dot(weight_gram_ref[...], back)
        square = exact_dot(back, mixed, (0, 0))
        done = (orthonormal if step == STEPS - 1 else conditioned)(works, back, mixed, square)
        image_work[...] = jnp.concatenate([d[1] for d in done], axis=1)
    back_work[...] = jnp.concatenate([d[0] for d in done], axis=1)
    image_out[...] = image_work[...]
    scaled = back_work[...] * math.sqrt(OUT)
    high = scaled.astype(jnp.bfloat16)
    pieces_out[:, :rank] = high
    pieces_out[:, rank:] = (scaled - high.astype(jnp.float32)).astype(jnp.bfloat16)


def chain(packed, width, rank):
    return pl.pallas_call(
        chain_kernel,
        out_shape=(jax.ShapeDtypeStruct((width, rank), jnp.float32), jax.ShapeDtypeStruct((width, 2 * rank), jnp.bfloat16)),
        in_specs=[pl.BlockSpec(memory_space=pltpu.VMEM)],
        out_specs=(pl.BlockSpec(memory_space=pltpu.VMEM),) * 2,
        scratch_shapes=[
            pltpu.VMEM((width, width), jnp.float32),
            pltpu.VMEM((width, rank), jnp.float32),
            pltpu.VMEM((width, rank), jnp.float32),
        ] + [pltpu.VMEM((BLOCK, 2 * BLOCK), jnp.float32)] * (rank // BLOCK),
        compiler_params=pltpu.CompilerParams(vmem_limit_bytes=48 * 2**20),
        name="chain",
    )(packed)


def basis_kernel(together, picks, pieces, *refs):
    weights, out = refs[:together], refs[together]
    rank = out.shape[1]
    for k, weight in enumerate(weights):
        both = lax.dot_general(weight[0], pieces[...], (((0,), (0,)), ((), ())), preferred_element_type=jnp.float32)
        out[k * HEAD_OUT:(k + 1) * HEAD_OUT, :] = both[:, :rank] + both[:, rank:]


def back_projected(picks, pieces, weights):
    width = pieces.shape[0]
    rank = pieces.shape[1] // 2
    heads_here = picks.shape[0]
    together = math.gcd(heads_here, 4)
    return pl.pallas_call(
        functools.partial(basis_kernel, together),
        out_shape=jax.ShapeDtypeStruct((heads_here * HEAD_OUT, rank), jnp.float32),
        grid_spec=pltpu.PrefetchScalarGridSpec(
            num_scalar_prefetch=1,
            grid=(heads_here // together,),
            in_specs=[pl.BlockSpec(pieces.shape, lambda at, picks: (0, 0))] + weight_specs(together, width),
            out_specs=pl.BlockSpec((together * HEAD_OUT, rank), lambda at, picks: (at, 0)),
        ),
        compiler_params=pltpu.CompilerParams(vmem_limit_bytes=48 * 2**20),
        name="back_projected",
    )(picks, pieces, *[weights] * together)


def on_device(latents, weights, start_basis, layer_pick):
    act = latents[0]
    width = act.shape[1]
    rank = start_basis.shape[1]
    heads_here = weights.shape[2] // HEAD_OUT
    slot = lax.axis_index("col")
    first_head = lax.axis_index(("tok", "head")) * heads_here
    picks = lax.dynamic_slice(layer_pick, (slot, first_head), (1, heads_here))[0]
    unit = 16 * lax.axis_size("tok")
    rows = -(-(width + 4 * HALF + 2) // unit) * unit
    packed = summed(local_sums(picks, act, start_basis, weights, rows))
    core, pieces = chain(packed, width, rank)
    return (back_projected(picks, pieces, weights)[None], core[None])


def solution(mesh):
    return jax.shard_map(
        on_device,
        mesh=mesh,
        in_specs=(
            P(("groups", "col"), ("tok", "head"), None),
            P(None, None, ("tok", "head")),
            P(("tok", "head"), None),
            P("groups", None),
        ),
        out_specs=(P(("groups", "col"), ("tok", "head"), None), P(("groups", "col"), None, None)),
        check_vma=False,
    )
```
